512 devices in a mesh: tm: 64 (over x, y, core), space: 8 (over z).
Axes of the slice: x: 4, y: 8, z: 8, core: 2. Of those that a mesh axis runs over, the one named last changes fastest.
Arguments:
- initial: float32 [16, 128, 128], P('space'), may hold values from -6 to 6
- conductivity: float32 [16, 128, 128], P('space'), may hold values from 0.1 to 1
- source: float32 [128, 16, 128, 128], P('tm', 'space'), may hold values from -4 to 4
Outputs:
- states: float32 [128, 16, 128, 128], P('tm', 'space')
The draws below stay inside these ranges and needn't reach their ends.
All inputs are finite; a program needn't handle non-finite values.
Results may differ from the reference program's by a relative error of at most 0.00002.
Values sent between devices are 32-bit elements; how exact they have to be, the bound alone decides.
A program may use at most 64 MiB of HBM per device.

```python
import math
import jax
import jax.numpy as jnp
from jax import lax

NX = 128
NY = 128
CF = 8
ITERS = 2
NZ = 16
STEPS = 128
NCOARSE = 16


def level_of(stream_key, extent, cuts, smallest, high):
    factor_of = 1.0
    for axis_at, parts in cuts:
        heights = jax.random.uniform(jax.random.fold_in(jax.random.fold_in(stream_key, 6), axis_at), (parts,), jnp.float32, smallest / len(cuts), high / len(cuts))
        factor_of = factor_of * jnp.repeat(jnp.exp(heights), extent[axis_at] // parts).reshape((-1,) + (1,) * (len(extent) - 1 - axis_at))
    return factor_of


def normal_values(stream_key, extent, deviation, reach, split=(), held_as=jnp.bfloat16):
    drawn = deviation * jax.random.normal(stream_key, extent, jnp.float32)
    if split:
        drawn = drawn * level_of(stream_key, extent, split, -0.22, 0.18)
    return jnp.clip(drawn, -reach, reach).astype(held_as)


def setup_inputs(seed: int = 0) -> dict:
    streams_of = jax.random.split(jax.random.key(seed), 4)
    return {
        "initial": normal_values(streams_of[0], (NZ, NX, NY), 1.0, 6.0, ((0, 8),), jnp.float32),
        "conductivity": jnp.clip(jnp.exp(math.log(1.0) - 2.3025851 * jax.random.uniform(streams_of[1], (NZ, NX, NY), jnp.float32) ** level_of(streams_of[1], (NZ, NX, NY), ((0, 8),), -0.2, 0.2)), 0.1, 1.0),
        "source": normal_values(streams_of[2], (STEPS, NZ, NX, NY), 0.3, 4.0, ((0, 64), (1, 8)), jnp.float32),
    }


fine_rate = 0.02


def shifted(padded, step_z, step_x, step_y):
    depth, rows, cols = padded.shape
    return padded[1 + step_z:depth - 1 + step_z, 1 + step_x:rows - 1 + step_x, 1 + step_y:cols - 1 + step_y]


def diffuse(field, cond, forcing, first_plane, speed, total):
    widen = ((0, 0), (1, 1), (1, 1))
    field_pad = jnp.pad(field, widen)
    cond_pad = jnp.pad(cond, widen)
    center = shifted(field_pad, 0, 0, 0)
    kcenter = shifted(cond_pad, 0, 0, 0)
    flux = jnp.zeros_like(center)
    for offset in ((1, 0, 0), (-1, 0, 0), (0, 1, 0), (0, -1, 0), (0, 0, 1), (0, 0, -1)):
        neighbour = shifted(field_pad, offset[0], offset[1], offset[2])
        kneighbour = shifted(cond_pad, offset[0], offset[1], offset[2])
        flux = flux + 0.5 * (kcenter + kneighbour) * (neighbour - center)
    updated = center + speed * flux + forcing
    index = first_plane + 1 + jnp.arange(field.shape[0] - 2, dtype=jnp.int32)
    inside = (index >= 0) & (index < total)
    return jnp.where(inside[:, None, None], updated, jnp.float32(0.0))


def reference(initial, conductivity, source):
    along = ((1, 1), (0, 0), (0, 0))
    cond_pad = jnp.pad(conductivity, along)

    def fine_step(state, forcing):
        updated = diffuse(jnp.pad(state, along), cond_pad, forcing, -1, fine_rate, NZ)
        return updated, updated

    def propagate(start, interval):
        final, series = lax.scan(fine_step, start, source[interval * CF:(interval + 1) * CF])
        return series

    def coarse(error):
        return diffuse(jnp.pad(error, along), cond_pad, jnp.float32(0.0), -1, fine_rate * CF, NZ)

    starts = [jnp.zeros_like(initial)] * NCOARSE
    for sweep in range(ITERS):
        ends = [propagate(starts[interval], interval)[-1] for interval in range(NCOARSE)]
        relaxed = [initial] + ends[:-1]
        ends = [propagate(relaxed[interval], interval)[-1] for interval in range(NCOARSE)]
        error = jnp.zeros_like(initial)
        starts = [initial]
        for interval in range(1, NCOARSE):
            error = coarse(error) + (ends[interval - 1] - relaxed[interval])
            starts.append(relaxed[interval] + error)
    return jnp.concatenate([propagate(starts[interval], interval) for interval in range(NCOARSE)], axis=0)
```

```python
import functools

import jax
import jax.numpy as jnp
from jax import lax
from jax.experimental import pallas as pl
from jax.experimental.pallas import tpu as pltpu
from jax.sharding import PartitionSpec as P

MESH = pl.DeviceIdType.MESH
F32 = jnp.float32
ROWS = 8
WIDE = 3 * ROWS
CHUNK = 4
LAGS = 16


def chunks(low, high):
    at = low
    while at < high:
        yield at, min(at + CHUNK, high)
        at += CHUNK


def kernel(intervals, depth, initial, cond, source, out, land_s, land_k, land_u, kx, sx, coef_a, coef_c, diag_a, diag_c,
           zed_a, zed_c, ping, pong, gsum, pair_in, v_mine, v_in, base, gam, dif, gam_w, dif_w, mixed, slots, start,
           middle, out_send, sem_s, sem_k, sem_u, sem_h, sem_p, sem_v, sem_m, sem_d, sem_o):
    tm = lax.axis_index("tm")
    z = lax.axis_index("space")
    interval = tm // 4
    quarter = tm % 4
    side = quarter // 2
    core = quarter % 2
    block = 2 * z + core
    first = interval == intervals - 1
    item = lax.rem(interval + 1, intervals)
    blocks = 2 * depth
    left = (tm - core + (1 - core), lax.rem(z + depth - (1 - core), depth))
    right = (tm - core + (1 - core), lax.rem(z + core, depth))
    pair_tm = tm - 2 * side + 2 * (1 - side)
    pair = (pair_tm, z)
    cross_tm = pair_tm - core + (1 - core)
    chip_tm = tm - core

    def interval_tm(which):
        return 4 * which + quarter

    barrier = pltpu.get_barrier_semaphore()

    def greet(device):
        pl.semaphore_signal(barrier, inc=1, device_id=device, device_id_type=MESH)

    partners = 0
    for step in range(depth):
        other = lax.rem(z + step, depth)
        greet((tm - core + (1 - core), other))
        partners += 1
        if step:
            greet((tm, other))
            partners += 1
    greet(pair)
    greet((cross_tm, left[1]))
    greet((cross_tm, right[1]))
    partners += 3
    for step in range(1, intervals):
        greet((interval_tm(lax.rem(interval + step, intervals)), z))
        partners += 1
    pl.semaphore_wait(barrier, partners)

    def send(src, dst, sems, k, device):
        pltpu.make_async_remote_copy(
            src_ref=src, dst_ref=dst, send_sem=sems.at[0, k], recv_sem=sems.at[1, k], device_id=device, device_id_type=MESH
        ).start()

    def take(ref, sems, k, way=1):
        pltpu.make_async_copy(ref, ref, sems.at[way, k]).wait()

    def spread(whole, land, sems):
        for step in range(1, depth):
            other = lax.rem(z + step, depth)
            rows = pl.ds(pl.multiple_of((2 * other + core) * ROWS, ROWS), ROWS)
            send(whole.at[:, rows], land.at[z], sems, 0, (tm, other))
        rows = pl.ds(pl.multiple_of(block * ROWS, ROWS), ROWS)
        pltpu.make_async_copy(whole.at[:, rows], land.at[z], sems.at[1, 0]).start()

    spread(cond, land_k, sem_k)
    for step in range(depth):
        other = lax.rem(z + step, depth)
        for flip in range(2):
            if step == 0 and flip == 0:
                continue
            goal = core if flip == 0 else 1 - core
            rows = pl.ds(pl.multiple_of((2 * other + goal) * ROWS, ROWS), ROWS)
            send(source.at[:, :, rows], land_s.at[core * depth + z], sem_s, 0, (chip_tm + goal, other))
    rows = pl.ds(pl.multiple_of(block * ROWS, ROWS), ROWS)
    pltpu.make_async_copy(source.at[:, :, rows], land_s.at[core * depth + z], sem_s.at[1, 0]).start()

    @pl.when(first)
    def _():
        spread(initial, land_u, sem_u)

    def gathered(land, row, parity, base_row, stride):
        flat = land.reshape(land.size // 128, 128)
        return flat[pl.ds(base_row + parity * ROWS + row, 8, stride=stride), :]

    own = pl.ds(ROWS, ROWS)

    def halo(field, sems, k, rows=ROWS):
        send(field.at[pl.ds(ROWS, rows)], field.at[pl.ds(2 * ROWS, rows)], sems, 2 * k, left)
        send(field.at[pl.ds(2 * ROWS - rows, rows)], field.at[pl.ds(ROWS - rows, rows)], sems, 2 * k + 1, right)

    def halo_take(field, sems, k, rows=ROWS, way=1):
        take(field.at[pl.ds(2 * ROWS, rows)], sems, 2 * k, way)
        take(field.at[pl.ds(ROWS - rows, rows)], sems, 2 * k + 1, way)

    take(land_k, sem_k, 0)
    for row in range(ROWS):
        for parity in range(2):
            kx[ROWS + row, parity] = gathered(land_k, row, parity, 0, 2 * ROWS)
    halo(kx, sem_h, 0)

    take(land_s, sem_s, 0)
    for pick in range(4):
        for row in range(ROWS):
            for parity in range(2):
                sx[pick, ROWS + row, parity] = gathered(
                    land_s, row, parity, (pick // 2) * depth * 4 * ROWS + (pick % 2) * 2 * ROWS, 4 * ROWS
                )
    for pick in range(4):
        halo(sx.at[pick], sem_h, 1 + pick, ROWS - 1 - pick)

    halo_take(kx, sem_h, 0)
    lane = lax.broadcasted_iota(jnp.int32, (8, 128), 1)
    sub = lax.broadcasted_iota(jnp.int32, (8, 128), 0)
    low_edge = block == 0
    high_edge = block == blocks - 1

    def kof(row, parity):
        value = kx[row, parity]
        if row < ROWS:
            value = jnp.where(low_edge, F32(0.0), value)
        if row >= 2 * ROWS:
            value = jnp.where(high_edge, F32(0.0), value)
        return value

    half = F32(0.01)
    zero = F32(0.0)
    for row in range(WIDE - 1):
        k0, k1 = kof(row, 0), kof(row, 1)
        za = half * (k0 + k1)
        zb_all = half * (k1 + jnp.where(sub == 7, zero, pltpu.roll(k0, 7, 0)))
        zb_off = jnp.where(sub == 7, zero, zb_all)
        zc_all = half * (k0 + jnp.where(sub == 0, zero, pltpu.roll(k1, 1, 0)))
        zc_off = jnp.where(sub == 0, zero, zc_all)
        zed_a[row, 0], zed_a[row, 1], zed_a[row, 2] = za, zc_off, zb_off
        zed_c[row, 0], zed_c[row, 1], zed_c[row, 2] = 8.0 * za, 8.0 * zc_off, 8.0 * zb_off
        for parity, here in enumerate((k0, k1)):
            up_all = half * (here + kof(row + 1, parity))
            up_off = up_all
            if row == ROWS - 1:
                up_off = jnp.where(low_edge, zero, up_all)
            if row == 2 * ROWS - 1:
                up_off = jnp.where(high_edge, zero, up_all)
            yp_all = half * (here + jnp.where(lane == 127, zero, pltpu.roll(here, 127, 1)))
            yp_off = jnp.where(lane == 127, zero, yp_all)
            ym_all = half * (here + jnp.where(lane == 0, zero, pltpu.roll(here, 1, 1)))
            ym_off = jnp.where(lane == 0, zero, ym_all)
            coef_a[0, row, parity], coef_c[0, row, parity] = up_off, 8.0 * up_off
            if row:
                down_all = half * (here + kof(row - 1, parity))
                total = (za + (zc_all if parity == 0 else zb_all)) + (yp_all + ym_all) + (up_all + down_all)
                coef_a[1, row, parity], coef_c[1, row, parity] = yp_off, 8.0 * yp_off
                coef_a[2, row, parity], coef_c[2, row, parity] = ym_off, 8.0 * ym_off
                diag_a[row, parity], diag_c[row, parity] = 1.0 - total, 1.0 - 8.0 * total

    fine = (coef_a, diag_a, zed_a)
    coarse = (coef_c, diag_c, zed_c)

    def stencil(ops, src, a, b):
        coef, diag, zed = ops
        n = b - a
        here = [src[pl.ds(a, n), parity] for parity in range(2)]
        outs = []
        for parity in range(2):
            u = here[parity]
            across = here[1 - parity]
            turned = pltpu.roll(across, 1 if parity == 0 else 7, 1)
            vert = zed[pl.ds(a, n), 0] * across + zed[pl.ds(a, n), 1 + parity] * turned
            rows = coef[0, pl.ds(a, n), parity] * src[pl.ds(a + 1, n), parity] \
                + coef[0, pl.ds(a - 1, n), parity] * src[pl.ds(a - 1, n), parity]
            cols = coef[1, pl.ds(a, n), parity] * pltpu.roll(u, 127, 2) + coef[2, pl.ds(a, n), parity] * pltpu.roll(u, 1, 2)
            outs.append((diag[pl.ds(a, n), parity] * u + rows) + (vert + cols))
        return outs

    def apply(ops, src, dst, low, high, forcing=None):
        for a, b in chunks(low, high):
            outs = stencil(ops, src, a, b)
            for parity in range(2):
                value = outs[parity]
                if forcing is not None:
                    value = value + forcing[pl.ds(a, b - a), parity]
                dst[pl.ds(a, b - a), parity] = value

    def run(ops, src, dst, steps, reach, spare):
        current = src
        for step in range(steps):
            reach -= 1
            goal = dst if step == steps - 1 else spare[step % 2]
            apply(ops, current, goal, ROWS - reach, 2 * ROWS + reach)
            current = goal

    spare = (ping, pong)

    for pick in range(4):
        halo_take(sx.at[pick], sem_h, 1 + pick, ROWS - 1 - pick)
    apply(fine, sx.at[0], ping, 2, 22, sx.at[1])
    apply(fine, ping, pong, 3, 21, sx.at[2])
    apply(fine, pong, v_mine, 4, 20, sx.at[3])
    run(fine, v_mine, gsum, 4, 4, spare)

    @pl.when(side == 1)
    def _():
        gsum[own] = v_mine[own]

    send(gsum.at[own], pair_in, sem_p, 0, pair)

    @pl.when(side == 0)
    def _():
        send(v_mine.at[pl.ds(4, 16)], v_in.at[pl.ds(4, 16)], sem_v, 0, pair)

    take(pair_in, sem_p, 0)

    @pl.when(first)
    def _():
        take(land_u, sem_u, 0)
        for row in range(ROWS):
            for parity in range(2):
                base[0, ROWS + row, parity] = gathered(land_u, row, parity, 0, 2 * ROWS)

    @pl.when(jnp.logical_not(first))
    def _():
        base[0, own] = gsum[own] + pair_in[...]

    mine = pl.ds(ROWS + 4 * side, 4)

    def post(n, src):
        @pl.when(item + n < intervals)
        def _():
            send(src, slots.at[n], sem_m, n, (interval_tm(item + n), z))

    for power in range(3):
        halo(base.at[power], sem_h, 5 + power)
        post(power, base.at[power, mine])
        halo_take(base.at[power], sem_h, 5 + power)
        if power < 2:
            run(fine, base.at[power], base.at[power + 1], 8, 8, spare)
    apply(coarse, base.at[2], dif.at[0], ROWS, 2 * ROWS)
    run(fine, base.at[2], gam.at[0], 8, 8, spare)
    dif[0, own] = gam[0, own] - dif[0, own]

    for turn in range(13):
        at, inner = turn // 8, turn % 8
        if inner == 0:
            now_g, now_d = gam.at[at], dif.at[at]
            wide = 8 if at == 0 else 4
            halo(now_g, sem_h, 8 + 2 * at, wide)
            halo(now_d, sem_h, 9 + 2 * at, wide)
        if turn == 0:
            post(3, now_g.at[mine])
        else:
            mixed[turn] = now_g[mine] + F32(turn) * now_d[mine]
            if turn < 12:
                post(3 + turn, mixed.at[turn])
        if inner == 0:
            halo_take(now_g, sem_h, 8 + 2 * at, wide)
            halo_take(now_d, sem_h, 9 + 2 * at, wide)
            reach = wide
        if turn == 12:
            break
        reach -= 1
        last = inner == 7
        next_g = gam.at[at + 1] if last else gam_w.at[inner % 2]
        next_d = dif.at[at + 1] if last else dif_w.at[inner % 2]
        apply(coarse, now_g, next_g, ROWS - reach, 2 * ROWS + reach)
        apply(coarse, now_d, next_d, ROWS - reach, 2 * ROWS + reach)
        now_g, now_d = next_g, next_d

    start[mine] = jnp.where(first, mixed[12], jnp.zeros_like(mixed[12]))
    for n in range(LAGS - 1):
        @pl.when(n <= interval)
        def _():
            take(slots.at[n], sem_m, n)
            start[mine] = start[mine] + slots[n]

    below = pl.ds(4 * side, 4)
    above = pl.ds(2 * ROWS + 4 * side, 4)
    send(start.at[mine], start.at[mine], sem_d, 0, pair)
    send(start.at[mine], start.at[above], sem_d, 1, left)
    send(start.at[mine], start.at[below], sem_d, 2, right)
    send(start.at[mine], start.at[above], sem_d, 3, (cross_tm, left[1]))
    send(start.at[mine], start.at[below], sem_d, 4, (cross_tm, right[1]))
    for k in range(5):
        take(slots.at[0], sem_d, k)

    run(fine, start, middle, 4, 8, spare)

    @pl.when(side == 0)
    def _():
        middle[pl.ds(4, 16)] = start[pl.ds(4, 16)]

    @pl.when(side == 1)
    def _():
        take(v_in.at[pl.ds(4, 16)], sem_v, 0)
        middle[pl.ds(4, 16)] = middle[pl.ds(4, 16)] + v_in[pl.ds(4, 16)]

    flat = out_send.reshape(out_send.size // 128, 128)
    current = middle
    my_rows = pl.ds(pl.multiple_of(block * ROWS, ROWS), ROWS)
    for pick in range(4):
        goal = spare[pick % 2]
        reach = 3 - pick
        apply(fine, current, goal, ROWS - reach, 2 * ROWS + reach, sx.at[pick])
        current = goal
        origin = (pick // 2) * depth * 4 * ROWS + (pick % 2) * 2 * ROWS
        for row in range(ROWS):
            for parity in range(2):
                flat[pl.ds(origin + parity * ROWS + row, 8, stride=4 * ROWS), :] = goal[ROWS + row, parity]
        if pick % 2:
            goal_core = pick // 2
            for step in range(1, depth):
                other = lax.rem(z + step, depth)
                send(out_send.at[goal_core, other], out.at[:, :, my_rows], sem_o, 0, (chip_tm + goal_core, other))

            @pl.when(core == goal_core)
            def _():
                pltpu.make_async_copy(out_send.at[goal_core, z], out.at[:, :, my_rows], sem_o.at[1, 0]).start()

            @pl.when(core != goal_core)
            def _():
                send(out_send.at[goal_core, z], out.at[:, :, my_rows], sem_o, 0, (chip_tm + goal_core, z))

    take(out, sem_o, 0)

    take(land_k.at[pl.ds(0, depth - 1)], sem_k, 0, 0)
    take(land_s.at[pl.ds(0, 2 * depth - 1)], sem_s, 0, 0)

    @pl.when(first)
    def _():
        take(land_u.at[pl.ds(0, depth - 1)], sem_u, 0, 0)

    @pl.when(side == 0)
    def _():
        take(v_in.at[pl.ds(4, 16)], sem_v, 0, 0)

    halo_take(kx, sem_h, 0, ROWS, 0)
    for pick in range(4):
        halo_take(sx.at[pick], sem_h, 1 + pick, ROWS - 1 - pick, 0)
    take(pair_in, sem_p, 0, 0)
    for power in range(3):
        halo_take(base.at[power], sem_h, 5 + power, ROWS, 0)
    for at, wide in ((0, 8), (1, 4)):
        halo_take(gam.at[at], sem_h, 8 + 2 * at, wide, 0)
        halo_take(dif.at[at], sem_h, 9 + 2 * at, wide, 0)
    for n in range(LAGS - 1):
        @pl.when(item + n < intervals)
        def _():
            take(slots.at[n], sem_m, n, 0)
    for k in range(5):
        take(slots.at[0], sem_d, k, 0)
    take(land_s.at[pl.ds(0, 2 * depth - 1)], sem_o, 0, 0)


def local(intervals, depth, initial, cond, source):
    def vm(*shape):
        return pltpu.VMEM(shape, F32)

    def field(*lead):
        return vm(*lead, WIDE, 2, 8, 128)

    dma = pltpu.SemaphoreType.DMA
    return pl.pallas_call(
        functools.partial(kernel, intervals, depth),
        out_shape=jax.ShapeDtypeStruct(source.shape, F32),
        in_specs=[pl.BlockSpec(memory_space=pl.ANY)] * 3,
        out_specs=pl.BlockSpec(memory_space=pl.ANY),
        scratch_shapes=[
            vm(2 * depth, 2, 2, ROWS, 128),
            vm(depth, 2, ROWS, 128),
            vm(depth, 2, ROWS, 128),
            field(),
            field(4),
            field(3),
            field(3),
            field(),
            field(),
            vm(WIDE, 3, 8, 128),
            vm(WIDE, 3, 8, 128),
            field(),
            field(),
            field(),
            vm(ROWS, 2, 8, 128),
            field(),
            field(),
            field(3),
            field(2),
            field(2),
            field(2),
            field(2),
            vm(13, 4, 2, 8, 128),
            vm(LAGS, 4, 2, 8, 128),
            field(),
            field(),
            vm(2, depth, 2, 2, ROWS, 128),
            dma((2, 1)),
            dma((2, 1)),
            dma((2, 1)),
            dma((2, 24)),
            dma((2, 1)),
            dma((2, 1)),
            dma((2, LAGS)),
            dma((2, 5)),
            dma((2, 1)),
        ],
        compiler_params=pltpu.CompilerParams(
            collective_id=0, has_side_effects=True, vmem_limit_bytes=40 * 1024 * 1024
        ),
        name="mgrit",
    )(initial, cond, source)


def solution(mesh):
    intervals = mesh.shape["tm"] // 4
    depth = mesh.shape["space"]
    return jax.shard_map(
        functools.partial(local, intervals, depth),
        mesh=mesh,
        in_specs=(P("space", None, None), P("space", None, None), P("tm", "space", None, None)),
        out_specs=P("tm", "space", None, None),
        check_vma=False,
    )
```

```python
import functools

import jax
import jax.numpy as jnp
from jax import lax
from jax.experimental import pallas as pl
from jax.experimental.pallas import tpu as pltpu
from jax.sharding import PartitionSpec as P

MESH = pl.DeviceIdType.MESH
F32 = jnp.float32
ROWS = 8
OWN = 2 * ROWS
WIDE = 5 * ROWS
CHUNK = 4
LAGS = 16


def chunks(low, high):
    at = low
    while at < high:
        yield at, min(at + CHUNK, high)
        at += CHUNK


def kernel(intervals, depth, initial, cond, source, out, land_s, land_k, land_u, kx, sx, coef_a, coef_c, diag_a, diag_c,
           zed_a, zed_c, ping, pong, gsum, pair_in, v_mine, v_in, base, gam, dif, gam_w, dif_w, mixed, slots, start,
           middle, out_send, sem_s, sem_k, sem_u, sem_h, sem_p, sem_v, sem_m, sem_d, sem_o):
    tm = lax.axis_index("tm")
    z = lax.axis_index("space")
    interval = tm // 4
    quarter = tm % 4
    side = quarter // 2
    core = quarter % 2
    block = 2 * z + core
    first = interval == intervals - 1
    item = lax.rem(interval + 1, intervals)
    blocks = 2 * depth
    left = (tm - core + (1 - core), lax.rem(z + depth - (1 - core), depth))
    right = (tm - core + (1 - core), lax.rem(z + core, depth))
    pair_tm = tm - 2 * side + 2 * (1 - side)
    pair = (pair_tm, z)
    cross_tm = pair_tm - core + (1 - core)
    chip_tm = tm - core

    def interval_tm(which):
        return 4 * which + quarter

    barrier = pltpu.get_barrier_semaphore()

    def greet(device):
        pl.semaphore_signal(barrier, inc=1, device_id=device, device_id_type=MESH)

    partners = 0
    for step in range(depth):
        other = lax.rem(z + step, depth)
        greet((tm - core + (1 - core), other))
        partners += 1
        if step:
            greet((tm, other))
            partners += 1
    greet(pair)
    greet((cross_tm, left[1]))
    greet((cross_tm, right[1]))
    partners += 3
    for step in range(1, intervals):
        greet((interval_tm(lax.rem(interval + step, intervals)), z))
        partners += 1
    pl.semaphore_wait(barrier, partners)

    def send(src, dst, sems, k, device):
        pltpu.make_async_remote_copy(
            src_ref=src, dst_ref=dst, send_sem=sems.at[0, k], recv_sem=sems.at[1, k], device_id=device, device_id_type=MESH
        ).start()

    def take(ref, sems, k, way=1):
        pltpu.make_async_copy(ref, ref, sems.at[way, k]).wait()

    def spread(whole, land, sems):
        for step in range(1, depth):
            other = lax.rem(z + step, depth)
            rows = pl.ds(pl.multiple_of((2 * other + core) * ROWS, ROWS), ROWS)
            send(whole.at[:, rows], land.at[z], sems, 0, (tm, other))
        rows = pl.ds(pl.multiple_of(block * ROWS, ROWS), ROWS)
        pltpu.make_async_copy(whole.at[:, rows], land.at[z], sems.at[1, 0]).start()

    spread(cond, land_k, sem_k)
    for step in range(depth):
        other = lax.rem(z + step, depth)
        for flip in range(2):
            if step == 0 and flip == 0:
                continue
            goal = core if flip == 0 else 1 - core
            rows = pl.ds(pl.multiple_of((2 * other + goal) * ROWS, ROWS), ROWS)
            send(source.at[:, :, rows], land_s.at[core * depth + z], sem_s, 0, (chip_tm + goal, other))
    rows = pl.ds(pl.multiple_of(block * ROWS, ROWS), ROWS)
    pltpu.make_async_copy(source.at[:, :, rows], land_s.at[core * depth + z], sem_s.at[1, 0]).start()

    @pl.when(first)
    def _():
        spread(initial, land_u, sem_u)

    def gathered(land, row, parity, base_row, stride):
        flat = land.reshape(land.size // 128, 128)
        return flat[pl.ds(base_row + parity * ROWS + row, 8, stride=stride), :]

    own = pl.ds(OWN, ROWS)
    left2 = (tm, lax.rem(z + depth - 1, depth))
    right2 = (tm, lax.rem(z + 1, depth))

    def halo(field, k, rows):
        send(field.at[pl.ds(OWN, rows)], field.at[pl.ds(OWN + ROWS, rows)], sem_h, k, left)
        send(field.at[pl.ds(OWN + ROWS - rows, rows)], field.at[pl.ds(OWN - rows, rows)], sem_h, k + 1, right)

    def halo_take(field, k, rows, way=1):
        take(field.at[pl.ds(OWN + ROWS, rows)], sem_h, k, way)
        take(field.at[pl.ds(OWN - rows, rows)], sem_h, k + 1, way)

    def wide_halo(field, k):
        for turn, (device, at) in enumerate(((left, 3), (right, 1), (left2, 4), (right2, 0))):
            send(field.at[own], field.at[pl.ds(at * ROWS, ROWS)], sem_h, k + turn, device)

    def wide_take(field, k, way=1):
        for turn, at in enumerate((3, 1, 4, 0)):
            take(field.at[pl.ds(at * ROWS, ROWS)], sem_h, k + turn, way)

    take(land_k, sem_k, 0)
    for row in range(ROWS):
        for parity in range(2):
            kx[OWN + row, parity] = gathered(land_k, row, parity, 0, 2 * ROWS)
    wide_halo(kx, 0)

    take(land_s, sem_s, 0)
    for pick in range(4):
        for row in range(ROWS):
            for parity in range(2):
                sx[pick, OWN + row, parity] = gathered(
                    land_s, row, parity, (pick // 2) * depth * 4 * ROWS + (pick % 2) * 2 * ROWS, 4 * ROWS
                )
    for pick in range(4):
        halo(sx.at[pick], 4 + 2 * pick, ROWS - 1 - pick)

    wide_take(kx, 0)
    lane = lax.broadcasted_iota(jnp.int32, (8, 128), 1)
    sub = lax.broadcasted_iota(jnp.int32, (8, 128), 0)
    low_edge = block == 0
    high_edge = block == blocks - 1

    def kof(row, parity):
        value = kx[row, parity]
        if row < OWN:
            value = jnp.where(low_edge if row >= ROWS else block <= 1, F32(0.0), value)
        if row >= OWN + ROWS:
            value = jnp.where(high_edge if row < OWN + 2 * ROWS else block >= blocks - 2, F32(0.0), value)
        return value

    half = F32(0.01)
    zero = F32(0.0)
    for row in range(WIDE - 1):
        k0, k1 = kof(row, 0), kof(row, 1)
        za = half * (k0 + k1)
        zb_all = half * (k1 + jnp.where(sub == 7, zero, pltpu.roll(k0, 7, 0)))
        zb_off = jnp.where(sub == 7, zero, zb_all)
        zc_all = half * (k0 + jnp.where(sub == 0, zero, pltpu.roll(k1, 1, 0)))
        zc_off = jnp.where(sub == 0, zero, zc_all)
        zed_a[row, 0], zed_a[row, 1], zed_a[row, 2] = za, zc_off, zb_off
        zed_c[row, 0], zed_c[row, 1], zed_c[row, 2] = 8.0 * za, 8.0 * zc_off, 8.0 * zb_off
        for parity, here in enumerate((k0, k1)):
            up_all = half * (here + kof(row + 1, parity))
            up_off = up_all
            for edge, at in ((block == 1, 1), (low_edge, 2), (high_edge, 3), (block == blocks - 2, 4)):
                if row == at * ROWS - 1:
                    up_off = jnp.where(edge, zero, up_all)
            yp_all = half * (here + jnp.where(lane == 127, zero, pltpu.roll(here, 127, 1)))
            yp_off = jnp.where(lane == 127, zero, yp_all)
            ym_all = half * (here + jnp.where(lane == 0, zero, pltpu.roll(here, 1, 1)))
            ym_off = jnp.where(lane == 0, zero, ym_all)
            coef_a[0, row, parity], coef_c[0, row, parity] = up_off, 8.0 * up_off
            if row:
                down_all = half * (here + kof(row - 1, parity))
                total = (za + (zc_all if parity == 0 else zb_all)) + (yp_all + ym_all) + (up_all + down_all)
                coef_a[1, row, parity], coef_c[1, row, parity] = yp_off, 8.0 * yp_off
                coef_a[2, row, parity], coef_c[2, row, parity] = ym_off, 8.0 * ym_off
                diag_a[row, parity], diag_c[row, parity] = 1.0 - total, 1.0 - 8.0 * total

    fine = (coef_a, diag_a, zed_a)
    coarse = (coef_c, diag_c, zed_c)

    def stencil(ops, src, a, b):
        coef, diag, zed = ops
        n = b - a
        here = [src[pl.ds(a, n), parity] for parity in range(2)]
        outs = []
        for parity in range(2):
            u = here[parity]
            across = here[1 - parity]
            turned = pltpu.roll(across, 1 if parity == 0 else 7, 1)
            vert = zed[pl.ds(a, n), 0] * across + zed[pl.ds(a, n), 1 + parity] * turned
            rows = coef[0, pl.ds(a, n), parity] * src[pl.ds(a + 1, n), parity] \
                + coef[0, pl.ds(a - 1, n), parity] * src[pl.ds(a - 1, n), parity]
            cols = coef[1, pl.ds(a, n), parity] * pltpu.roll(u, 127, 2) + coef[2, pl.ds(a, n), parity] * pltpu.roll(u, 1, 2)
            outs.append((diag[pl.ds(a, n), parity] * u + rows) + (vert + cols))
        return outs

    def apply(ops, src, dst, low, high, forcing=None):
        for a, b in chunks(low, high):
            outs = stencil(ops, src, a, b)
            for parity in range(2):
                value = outs[parity]
                if forcing is not None:
                    value = value + forcing[pl.ds(a, b - a), parity]
                dst[pl.ds(a, b - a), parity] = value

    def run(ops, src, dst, steps, reach, spare):
        current = src
        for step in range(steps):
            reach -= 1
            goal = dst if step == steps - 1 else spare[step % 2]
            apply(ops, current, goal, OWN - reach, OWN + ROWS + reach)
            current = goal

    spare = (ping, pong)

    for pick in range(4):
        halo_take(sx.at[pick], 4 + 2 * pick, ROWS - 1 - pick)
    apply(fine, sx.at[0], ping, OWN - 6, OWN + ROWS + 6, sx.at[1])
    apply(fine, ping, pong, OWN - 5, OWN + ROWS + 5, sx.at[2])
    apply(fine, pong, v_mine, OWN - 4, OWN + ROWS + 4, sx.at[3])
    run(fine, v_mine, gsum, 4, 4, spare)

    @pl.when(side == 1)
    def _():
        gsum[own] = v_mine[own]

    @pl.when(first)
    def _():
        take(land_u, sem_u, 0)
        for row in range(ROWS):
            for parity in range(2):
                gsum[OWN + row, parity] = jnp.where(side == 0, gathered(land_u, row, parity, 0, 2 * ROWS), zero)

    send(gsum.at[own], pair_in.at[own], sem_p, 0, pair)
    take(pair_in.at[own], sem_p, 0)
    base[0, own] = gsum[own] + pair_in[own]
    wide_halo(base.at[0], 12)

    mine = pl.ds(OWN + 4 * side, 4)

    def post(n, src):
        @pl.when(item + n < intervals)
        def _():
            send(src, slots.at[n], sem_m, n, (interval_tm(item + n), z))

    post(0, base.at[0, mine])
    wide_take(base.at[0], 12)
    run(fine, base.at[0], base.at[1], 8, 16, spare)
    post(1, base.at[1, mine])
    run(fine, base.at[1], base.at[2], 8, 8, spare)
    wide_halo(base.at[2], 16)
    post(2, base.at[2, mine])

    @pl.when(side == 0)
    def _():
        send(v_mine.at[pl.ds(OWN - 4, 16)], v_in.at[pl.ds(OWN - 4, 16)], sem_v, 0, pair)

    wide_take(base.at[2], 16)
    apply(coarse, base.at[2], dif.at[0], OWN - ROWS, OWN + 2 * ROWS)
    run(fine, base.at[2], gam.at[0], 8, 16, spare)
    inner_rows = pl.ds(OWN - ROWS, 3 * ROWS)
    dif[0, inner_rows] = gam[0, inner_rows] - dif[0, inner_rows]

    for turn in range(13):
        at, inner = turn // 8, turn % 8
        if inner == 0:
            now_g, now_d = gam.at[at], dif.at[at]
            reach = 8
            if at:
                reach = 4
                halo(now_g, 20, reach)
                halo(now_d, 22, reach)
        if turn == 0:
            post(3, now_g.at[mine])
        else:
            mixed[turn] = now_g[mine] + F32(turn) * now_d[mine]
            if turn < 12:
                post(3 + turn, mixed.at[turn])
        if inner == 0 and at:
            halo_take(now_g, 20, reach)
            halo_take(now_d, 22, reach)
        if turn == 12:
            break
        reach -= 1
        last = inner == 7
        next_g = gam.at[at + 1] if last else gam_w.at[inner % 2]
        next_d = dif.at[at + 1] if last else dif_w.at[inner % 2]
        apply(coarse, now_g, next_g, OWN - reach, OWN + ROWS + reach)
        apply(coarse, now_d, next_d, OWN - reach, OWN + ROWS + reach)
        now_g, now_d = next_g, next_d

    start[mine] = jnp.where(first, mixed[12], jnp.zeros_like(mixed[12]))
    for n in range(LAGS - 1):
        @pl.when(n <= interval)
        def _():
            take(slots.at[n], sem_m, n)
            start[mine] = start[mine] + slots[n]

    below = pl.ds(OWN - ROWS + 4 * side, 4)
    above = pl.ds(OWN + ROWS + 4 * side, 4)
    send(start.at[mine], start.at[mine], sem_d, 0, pair)
    send(start.at[mine], start.at[above], sem_d, 1, left)
    send(start.at[mine], start.at[below], sem_d, 2, right)
    send(start.at[mine], start.at[above], sem_d, 3, (cross_tm, left[1]))
    send(start.at[mine], start.at[below], sem_d, 4, (cross_tm, right[1]))
    for k in range(5):
        take(slots.at[0], sem_d, k)

    run(fine, start, middle, 4, 8, spare)

    @pl.when(side == 0)
    def _():
        middle[pl.ds(OWN - 4, 16)] = start[pl.ds(OWN - 4, 16)]

    @pl.when(side == 1)
    def _():
        take(v_in.at[pl.ds(OWN - 4, 16)], sem_v, 0)
        middle[pl.ds(OWN - 4, 16)] = middle[pl.ds(OWN - 4, 16)] + v_in[pl.ds(OWN - 4, 16)]

    flat = out_send.reshape(out_send.size // 128, 128)
    current = middle
    my_rows = pl.ds(pl.multiple_of(block * ROWS, ROWS), ROWS)
    for pick in range(4):
        goal = spare[pick % 2]
        reach = 3 - pick
        apply(fine, current, goal, OWN - reach, OWN + ROWS + reach, sx.at[pick])
        current = goal
        origin = (pick // 2) * depth * 4 * ROWS + (pick % 2) * 2 * ROWS
        for row in range(ROWS):
            for parity in range(2):
                flat[pl.ds(origin + parity * ROWS + row, 8, stride=4 * ROWS), :] = goal[OWN + row, parity]
        if pick % 2:
            goal_core = pick // 2
            for step in range(1, depth):
                other = lax.rem(z + step, depth)
                send(out_send.at[goal_core, other], out.at[:, :, my_rows], sem_o, 0, (chip_tm + goal_core, other))

            @pl.when(core == goal_core)
            def _():
                pltpu.make_async_copy(out_send.at[goal_core, z], out.at[:, :, my_rows], sem_o.at[1, 0]).start()

            @pl.when(core != goal_core)
            def _():
                send(out_send.at[goal_core, z], out.at[:, :, my_rows], sem_o, 0, (chip_tm + goal_core, z))

    take(land_k.at[pl.ds(0, depth - 1)], sem_k, 0, 0)
    take(land_s.at[pl.ds(0, 2 * depth - 1)], sem_s, 0, 0)

    @pl.when(first)
    def _():
        take(land_u.at[pl.ds(0, depth - 1)], sem_u, 0, 0)

    @pl.when(side == 0)
    def _():
        take(v_in.at[pl.ds(OWN - 4, 16)], sem_v, 0, 0)

    wide_take(kx, 0, 0)
    for pick in range(4):
        halo_take(sx.at[pick], 4 + 2 * pick, ROWS - 1 - pick, 0)
    take(gsum.at[own], sem_p, 0, 0)
    wide_take(base.at[0], 12, 0)
    wide_take(base.at[2], 16, 0)
    halo_take(gam.at[1], 20, 4, 0)
    halo_take(dif.at[1], 22, 4, 0)
    for n in range(LAGS - 1):
        @pl.when(item + n < intervals)
        def _():
            take(slots.at[n], sem_m, n, 0)
    for k in range(5):
        take(slots.at[0], sem_d, k, 0)
    take(land_s.at[pl.ds(0, 2 * depth - 1)], sem_o, 0, 0)
    take(out, sem_o, 0)


def local(intervals, depth, initial, cond, source):
    def vm(*shape):
        return pltpu.VMEM(shape, F32)

    def field(*lead):
        return vm(*lead, WIDE, 2, 8, 128)

    dma = pltpu.SemaphoreType.DMA
    return pl.pallas_call(
        functools.partial(kernel, intervals, depth),
        out_shape=jax.ShapeDtypeStruct(source.shape, F32),
        in_specs=[pl.BlockSpec(memory_space=pl.ANY)] * 3,
        out_specs=pl.BlockSpec(memory_space=pl.ANY),
        scratch_shapes=[
            vm(2 * depth, 2, 2, ROWS, 128),
            vm(depth, 2, ROWS, 128),
            vm(depth, 2, ROWS, 128),
            field(),
            field(4),
            field(3),
            field(3),
            field(),
            field(),
            vm(WIDE, 3, 8, 128),
            vm(WIDE, 3, 8, 128),
            field(),
            field(),
            field(),
            field(),
            field(),
            field(),
            field(3),
            field(2),
            field(2),
            field(2),
            field(2),
            vm(13, 4, 2, 8, 128),
            vm(LAGS, 4, 2, 8, 128),
            field(),
            field(),
            vm(2, depth, 2, 2, ROWS, 128),
            dma((2, 1)),
            dma((2, 1)),
            dma((2, 1)),
            dma((2, 24)),
            dma((2, 5)),
            dma((2, 1)),
            dma((2, LAGS)),
            dma((2, 5)),
            dma((2, 1)),
        ],
        compiler_params=pltpu.CompilerParams(
            collective_id=0, has_side_effects=True, vmem_limit_bytes=60 * 1024 * 1024
        ),
        name="mgrit",
    )(initial, cond, source)


def solution(mesh):
    intervals = mesh.shape["tm"] // 4
    depth = mesh.shape["space"]
    return jax.shard_map(
        functools.partial(local, intervals, depth),
        mesh=mesh,
        in_specs=(P("space", None, None), P("space", None, None), P("tm", "space", None, None)),
        out_specs=P("tm", "space", None, None),
        check_vma=False,
    )
```

```python
import functools

import jax
import jax.numpy as jnp
from jax import lax
from jax.experimental import pallas as pl
from jax.experimental.pallas import tpu as pltpu
from jax.sharding import PartitionSpec as P

MESH = pl.DeviceIdType.MESH
F32 = jnp.float32
ROWS = 8
OWN = 2 * ROWS
WIDE = 5 * ROWS
CHUNK = 4
LAGS = 16


def chunks(low, high):
    at = low
    while at < high:
        yield at, min(at + CHUNK, high)
        at += CHUNK


def kernel(intervals, depth, far_initial, far_cond, far_source, out, initial, cond, source, land_s, land_k, land_u, kx, sx, coef_a, coef_c, diag_a, diag_c,
           zed_a, zed_c, ping, pong, gsum, pair_in, v_mine, v_in, base, gam, dif, gam_w, dif_w, mixed, slots, start,
           middle, out_send, sem_s, sem_k, sem_u, sem_h, sem_p, sem_v, sem_m, sem_d, sem_o, sem_i):
    tm = lax.axis_index("tm")
    z = lax.axis_index("space")
    interval = tm // 4
    quarter = tm % 4
    side = quarter // 2
    core = quarter % 2
    block = 2 * z + core
    first = interval == intervals - 1
    item = lax.rem(interval + 1, intervals)
    blocks = 2 * depth
    left = (tm - core + (1 - core), lax.rem(z + depth - (1 - core), depth))
    right = (tm - core + (1 - core), lax.rem(z + core, depth))
    pair_tm = tm - 2 * side + 2 * (1 - side)
    pair = (pair_tm, z)
    cross_tm = pair_tm - core + (1 - core)
    chip_tm = tm - core

    def interval_tm(which):
        return 4 * which + quarter

    fetches = [
        pltpu.make_async_copy(there, here, sem_i.at[k])
        for k, (there, here) in enumerate(((far_cond, cond), (far_source, source), (far_initial, initial)))
    ]
    for fetch in fetches:
        fetch.start()

    barrier = pltpu.get_barrier_semaphore()

    def greet(device):
        pl.semaphore_signal(barrier, inc=1, device_id=device, device_id_type=MESH)

    partners = 0
    for step in range(depth):
        other = lax.rem(z + step, depth)
        greet((tm - core + (1 - core), other))
        partners += 1
        if step:
            greet((tm, other))
            partners += 1
    greet(pair)
    greet((cross_tm, left[1]))
    greet((cross_tm, right[1]))
    partners += 3
    for step in range(1, intervals):
        greet((interval_tm(lax.rem(interval + step, intervals)), z))
        partners += 1
    for fetch in fetches:
        fetch.wait()
    pl.semaphore_wait(barrier, partners)

    def send(src, dst, sems, k, device):
        pltpu.make_async_remote_copy(
            src_ref=src, dst_ref=dst, send_sem=sems.at[0, k], recv_sem=sems.at[1, k], device_id=device, device_id_type=MESH
        ).start()

    def take(ref, sems, k, way=1):
        pltpu.make_async_copy(ref, ref, sems.at[way, k]).wait()

    def spread(whole, land, sems):
        for step in range(1, depth):
            other = lax.rem(z + step, depth)
            rows = pl.ds(pl.multiple_of((2 * other + core) * ROWS, ROWS), ROWS)
            send(whole.at[:, rows], land.at[z], sems, 0, (tm, other))
        rows = pl.ds(pl.multiple_of(block * ROWS, ROWS), ROWS)
        pltpu.make_async_copy(whole.at[:, rows], land.at[z], sems.at[1, 0]).start()

    spread(cond, land_k, sem_k)
    for step in range(depth):
        other = lax.rem(z + step, depth)
        for flip in range(2):
            if step == 0 and flip == 0:
                continue
            goal = core if flip == 0 else 1 - core
            rows = pl.ds(pl.multiple_of((2 * other + goal) * ROWS, ROWS), ROWS)
            send(source.at[:, :, rows], land_s.at[core * depth + z], sem_s, 0, (chip_tm + goal, other))
    rows = pl.ds(pl.multiple_of(block * ROWS, ROWS), ROWS)
    pltpu.make_async_copy(source.at[:, :, rows], land_s.at[core * depth + z], sem_s.at[1, 0]).start()

    @pl.when(first)
    def _():
        spread(initial, land_u, sem_u)

    def gathered(land, row, parity, base_row, stride):
        flat = land.reshape(land.size // 128, 128)
        return flat[pl.ds(base_row + parity * ROWS + row, 8, stride=stride), :]

    own = pl.ds(OWN, ROWS)
    left2 = (tm, lax.rem(z + depth - 1, depth))
    right2 = (tm, lax.rem(z + 1, depth))

    def halo(field, k, rows):
        send(field.at[pl.ds(OWN, rows)], field.at[pl.ds(OWN + ROWS, rows)], sem_h, k, left)
        send(field.at[pl.ds(OWN + ROWS - rows, rows)], field.at[pl.ds(OWN - rows, rows)], sem_h, k + 1, right)

    def halo_take(field, k, rows, way=1):
        take(field.at[pl.ds(OWN + ROWS, rows)], sem_h, k, way)
        take(field.at[pl.ds(OWN - rows, rows)], sem_h, k + 1, way)

    def wide_halo(field, k):
        for turn, (device, at) in enumerate(((left, 3), (right, 1), (left2, 4), (right2, 0))):
            send(field.at[own], field.at[pl.ds(at * ROWS, ROWS)], sem_h, k + turn, device)

    def wide_take(field, k, way=1):
        for turn, at in enumerate((3, 1, 4, 0)):
            take(field.at[pl.ds(at * ROWS, ROWS)], sem_h, k + turn, way)

    take(land_k, sem_k, 0)
    for row in range(ROWS):
        for parity in range(2):
            kx[OWN + row, parity] = gathered(land_k, row, parity, 0, 2 * ROWS)
    halo(kx, 0, ROWS)

    take(land_s, sem_s, 0)
    for pick in range(4):
        for row in range(ROWS):
            for parity in range(2):
                sx[pick, OWN + row, parity] = gathered(
                    land_s, row, parity, (pick // 2) * depth * 4 * ROWS + (pick % 2) * 2 * ROWS, 4 * ROWS
                )
    for pick in range(4):
        halo(sx.at[pick], 4 + 2 * pick, ROWS - 1 - pick)
    send(kx.at[own], kx.at[pl.ds(4 * ROWS, ROWS)], sem_h, 2, left2)
    send(kx.at[own], kx.at[pl.ds(0, ROWS)], sem_h, 3, right2)

    halo_take(kx, 0, ROWS)
    lane = lax.broadcasted_iota(jnp.int32, (8, 128), 1)
    sub = lax.broadcasted_iota(jnp.int32, (8, 128), 0)
    low_edge = block == 0
    high_edge = block == blocks - 1

    def kof(row, parity):
        value = kx[row, parity]
        if row < OWN:
            value = jnp.where(low_edge if row >= ROWS else block <= 1, F32(0.0), value)
        if row >= OWN + ROWS:
            value = jnp.where(high_edge if row < OWN + 2 * ROWS else block >= blocks - 2, F32(0.0), value)
        return value

    half = F32(0.01)
    zero = F32(0.0)
    def coefficients(row, below):
        k0, k1 = kof(row, 0), kof(row, 1)
        za = half * (k0 + k1)
        zb_all = half * (k1 + jnp.where(sub == 7, zero, pltpu.roll(k0, 7, 0)))
        zb_off = jnp.where(sub == 7, zero, zb_all)
        zc_all = half * (k0 + jnp.where(sub == 0, zero, pltpu.roll(k1, 1, 0)))
        zc_off = jnp.where(sub == 0, zero, zc_all)
        zed_a[row, 0], zed_a[row, 1], zed_a[row, 2] = za, zc_off, zb_off
        zed_c[row, 0], zed_c[row, 1], zed_c[row, 2] = 8.0 * za, 8.0 * zc_off, 8.0 * zb_off
        for parity, here in enumerate((k0, k1)):
            up_all = half * (here + kof(row + 1, parity))
            up_off = up_all
            for edge, at in ((block == 1, 1), (low_edge, 2), (high_edge, 3), (block == blocks - 2, 4)):
                if row == at * ROWS - 1:
                    up_off = jnp.where(edge, zero, up_all)
            yp_all = half * (here + jnp.where(lane == 127, zero, pltpu.roll(here, 127, 1)))
            yp_off = jnp.where(lane == 127, zero, yp_all)
            ym_all = half * (here + jnp.where(lane == 0, zero, pltpu.roll(here, 1, 1)))
            ym_off = jnp.where(lane == 0, zero, ym_all)
            coef_a[0, row, parity], coef_c[0, row, parity] = up_off, 8.0 * up_off
            if below:
                down_all = half * (here + kof(row - 1, parity))
                total = (za + (zc_all if parity == 0 else zb_all)) + (yp_all + ym_all) + (up_all + down_all)
                coef_a[1, row, parity], coef_c[1, row, parity] = yp_off, 8.0 * yp_off
                coef_a[2, row, parity], coef_c[2, row, parity] = ym_off, 8.0 * ym_off
                diag_a[row, parity], diag_c[row, parity] = 1.0 - total, 1.0 - 8.0 * total

    for row in range(ROWS, 4 * ROWS - 1):
        coefficients(row, row > ROWS)

    fine = (coef_a, diag_a, zed_a)
    coarse = (coef_c, diag_c, zed_c)

    def stencil(ops, src, a, b):
        coef, diag, zed = ops
        n = b - a
        here = [src[pl.ds(a, n), parity] for parity in range(2)]
        outs = []
        for parity in range(2):
            u = here[parity]
            across = here[1 - parity]
            turned = pltpu.roll(across, 1 if parity == 0 else 7, 1)
            vert = zed[pl.ds(a, n), 0] * across + zed[pl.ds(a, n), 1 + parity] * turned
            rows = coef[0, pl.ds(a, n), parity] * src[pl.ds(a + 1, n), parity] \
                + coef[0, pl.ds(a - 1, n), parity] * src[pl.ds(a - 1, n), parity]
            cols = coef[1, pl.ds(a, n), parity] * pltpu.roll(u, 127, 2) + coef[2, pl.ds(a, n), parity] * pltpu.roll(u, 1, 2)
            outs.append((diag[pl.ds(a, n), parity] * u + rows) + (vert + cols))
        return outs

    def apply(ops, src, dst, low, high, forcing=None):
        for a, b in chunks(low, high):
            outs = stencil(ops, src, a, b)
            for parity in range(2):
                value = outs[parity]
                if forcing is not None:
                    value = value + forcing[pl.ds(a, b - a), parity]
                dst[pl.ds(a, b - a), parity] = value

    def run(ops, src, dst, steps, reach, spare):
        current = src
        for step in range(steps):
            reach -= 1
            goal = dst if step == steps - 1 else spare[step % 2]
            apply(ops, current, goal, OWN - reach, OWN + ROWS + reach)
            current = goal

    spare = (ping, pong)

    for pick in range(4):
        halo_take(sx.at[pick], 4 + 2 * pick, ROWS - 1 - pick)
    apply(fine, sx.at[0], ping, OWN - 6, OWN + ROWS + 6, sx.at[1])
    apply(fine, ping, pong, OWN - 5, OWN + ROWS + 5, sx.at[2])
    apply(fine, pong, v_mine, OWN - 4, OWN + ROWS + 4, sx.at[3])
    run(fine, v_mine, gsum, 4, 4, spare)

    @pl.when(side == 1)
    def _():
        gsum[own] = v_mine[own]

    @pl.when(first)
    def _():
        take(land_u, sem_u, 0)
        for row in range(ROWS):
            for parity in range(2):
                gsum[OWN + row, parity] = jnp.where(side == 0, gathered(land_u, row, parity, 0, 2 * ROWS), zero)

    send(gsum.at[own], pair_in.at[own], sem_p, 0, pair)
    take(kx.at[pl.ds(4 * ROWS, ROWS)], sem_h, 2)
    take(kx.at[pl.ds(0, ROWS)], sem_h, 3)
    for row in (*range(ROWS + 1), *range(4 * ROWS - 1, WIDE - 1)):
        coefficients(row, row > 0)
    take(pair_in.at[own], sem_p, 0)
    base[0, own] = gsum[own] + pair_in[own]
    wide_halo(base.at[0], 12)

    mine = pl.ds(OWN + 4 * side, 4)

    def post(n, src):
        @pl.when(item + n < intervals)
        def _():
            send(src, slots.at[n], sem_m, n, (interval_tm(item + n), z))

    post(0, base.at[0, mine])
    wide_take(base.at[0], 12)
    run(fine, base.at[0], base.at[1], 8, 16, spare)
    post(1, base.at[1, mine])
    run(fine, base.at[1], base.at[2], 8, 8, spare)
    wide_halo(base.at[2], 16)
    post(2, base.at[2, mine])

    @pl.when(side == 0)
    def _():
        send(v_mine.at[pl.ds(OWN - 4, 16)], v_in.at[pl.ds(OWN - 4, 16)], sem_v, 0, pair)

    wide_take(base.at[2], 16)
    apply(coarse, base.at[2], dif.at[0], OWN - ROWS, OWN + 2 * ROWS)
    run(fine, base.at[2], gam.at[0], 8, 16, spare)
    inner_rows = pl.ds(OWN - ROWS, 3 * ROWS)
    dif[0, inner_rows] = gam[0, inner_rows] - dif[0, inner_rows]

    for turn in range(13):
        at, inner = turn // 8, turn % 8
        if inner == 0:
            now_g, now_d = gam.at[at], dif.at[at]
            reach = 8
            if at:
                reach = 4
                halo(now_g, 20, reach)
                halo(now_d, 22, reach)
        if turn == 0:
            post(3, now_g.at[mine])
        else:
            mixed[turn] = now_g[mine] + F32(turn) * now_d[mine]
            if turn < 12:
                post(3 + turn, mixed.at[turn])
        if inner == 0 and at:
            halo_take(now_g, 20, reach)
            halo_take(now_d, 22, reach)
        if turn == 12:
            break
        reach -= 1
        last = inner == 7
        next_g = gam.at[at + 1] if last else gam_w.at[inner % 2]
        next_d = dif.at[at + 1] if last else dif_w.at[inner % 2]
        apply(coarse, now_g, next_g, OWN - reach, OWN + ROWS + reach)
        apply(coarse, now_d, next_d, OWN - reach, OWN + ROWS + reach)
        now_g, now_d = next_g, next_d

    start[mine] = jnp.where(first, mixed[12], jnp.zeros_like(mixed[12]))
    for n in range(LAGS - 1):
        @pl.when(n <= interval)
        def _():
            take(slots.at[n], sem_m, n)
            start[mine] = start[mine] + slots[n]

    below = pl.ds(OWN - ROWS + 4 * side, 4)
    above = pl.ds(OWN + ROWS + 4 * side, 4)
    send(start.at[mine], start.at[mine], sem_d, 0, pair)
    send(start.at[mine], start.at[above], sem_d, 1, left)
    send(start.at[mine], start.at[below], sem_d, 2, right)
    send(start.at[mine], start.at[above], sem_d, 3, (cross_tm, left[1]))
    send(start.at[mine], start.at[below], sem_d, 4, (cross_tm, right[1]))
    for k in range(5):
        take(slots.at[0], sem_d, k)

    run(fine, start, middle, 4, 8, spare)

    @pl.when(side == 0)
    def _():
        middle[pl.ds(OWN - 4, 16)] = start[pl.ds(OWN - 4, 16)]

    @pl.when(side == 1)
    def _():
        take(v_in.at[pl.ds(OWN - 4, 16)], sem_v, 0)
        middle[pl.ds(OWN - 4, 16)] = middle[pl.ds(OWN - 4, 16)] + v_in[pl.ds(OWN - 4, 16)]

    flat = out_send.reshape(out_send.size // 128, 128)
    current = middle
    my_rows = pl.ds(pl.multiple_of(block * ROWS, ROWS), ROWS)
    for pick in range(4):
        goal = spare[pick % 2]
        reach = 3 - pick
        apply(fine, current, goal, OWN - reach, OWN + ROWS + reach, sx.at[pick])
        current = goal
        origin = (pick // 2) * depth * 4 * ROWS + (pick % 2) * 2 * ROWS
        for row in range(ROWS):
            for parity in range(2):
                flat[pl.ds(origin + parity * ROWS + row, 8, stride=4 * ROWS), :] = goal[OWN + row, parity]
        if pick % 2:
            goal_core = pick // 2
            for step in (4, 3, 5, 2, 6, 1, 7):
                other = lax.rem(z + step, depth)
                send(out_send.at[goal_core, other], out.at[:, :, my_rows], sem_o, 0, (chip_tm + goal_core, other))

            @pl.when(core == goal_core)
            def _():
                pltpu.make_async_copy(out_send.at[goal_core, z], out.at[:, :, my_rows], sem_o.at[1, 0]).start()

            @pl.when(core != goal_core)
            def _():
                send(out_send.at[goal_core, z], out.at[:, :, my_rows], sem_o, 0, (chip_tm + goal_core, z))

    take(land_k.at[pl.ds(0, depth - 1)], sem_k, 0, 0)
    take(land_s.at[pl.ds(0, 2 * depth - 1)], sem_s, 0, 0)

    @pl.when(first)
    def _():
        take(land_u.at[pl.ds(0, depth - 1)], sem_u, 0, 0)

    @pl.when(side == 0)
    def _():
        take(v_in.at[pl.ds(OWN - 4, 16)], sem_v, 0, 0)

    wide_take(kx, 0, 0)
    for pick in range(4):
        halo_take(sx.at[pick], 4 + 2 * pick, ROWS - 1 - pick, 0)
    take(gsum.at[own], sem_p, 0, 0)
    wide_take(base.at[0], 12, 0)
    wide_take(base.at[2], 16, 0)
    halo_take(gam.at[1], 20, 4, 0)
    halo_take(dif.at[1], 22, 4, 0)
    for n in range(LAGS - 1):
        @pl.when(item + n < intervals)
        def _():
            take(slots.at[n], sem_m, n, 0)
    for k in range(5):
        take(slots.at[0], sem_d, k, 0)
    take(land_s.at[pl.ds(0, 2 * depth - 1)], sem_o, 0, 0)
    take(out, sem_o, 0)


def local(intervals, depth, initial, cond, source):
    def vm(*shape):
        return pltpu.VMEM(shape, F32)

    def field(*lead):
        return vm(*lead, WIDE, 2, 8, 128)

    dma = pltpu.SemaphoreType.DMA
    return pl.pallas_call(
        functools.partial(kernel, intervals, depth),
        out_shape=jax.ShapeDtypeStruct(source.shape, F32),
        in_specs=[pl.BlockSpec(memory_space=pl.ANY)] * 3,
        out_specs=pl.BlockSpec(memory_space=pl.ANY),
        scratch_shapes=[
            vm(*initial.shape),
            vm(*cond.shape),
            vm(*source.shape),
            vm(2 * depth, 2, 2, ROWS, 128),
            vm(depth, 2, ROWS, 128),
            vm(depth, 2, ROWS, 128),
            field(),
            field(4),
            field(3),
            field(3),
            field(),
            field(),
            vm(WIDE, 3, 8, 128),
            vm(WIDE, 3, 8, 128),
            field(),
            field(),
            field(),
            field(),
            field(),
            field(),
            field(3),
            field(2),
            field(2),
            field(2),
            field(2),
            vm(13, 4, 2, 8, 128),
            vm(LAGS, 4, 2, 8, 128),
            field(),
            field(),
            vm(2, depth, 2, 2, ROWS, 128),
            dma((2, 1)),
            dma((2, 1)),
            dma((2, 1)),
            dma((2, 24)),
            dma((2, 5)),
            dma((2, 1)),
            dma((2, LAGS)),
            dma((2, 5)),
            dma((2, 1)),
            dma((3,)),
        ],
        compiler_params=pltpu.CompilerParams(
            collective_id=0, has_side_effects=True, vmem_limit_bytes=60 * 1024 * 1024
        ),
        name="mgrit",
    )(initial, cond, source)


def solution(mesh):
    intervals = mesh.shape["tm"] // 4
    depth = mesh.shape["space"]
    return jax.shard_map(
        functools.partial(local, intervals, depth),
        mesh=mesh,
        in_specs=(P("space", None, None), P("space", None, None), P("tm", "space", None, None)),
        out_specs=P("tm", "space", None, None),
        check_vma=False,
    )
```

```python
import functools

import jax
import jax.numpy as jnp
from jax import lax
from jax.experimental import pallas as pl
from jax.experimental.pallas import tpu as pltpu
from jax.sharding import PartitionSpec as P

MESH = pl.DeviceIdType.MESH
F32 = jnp.float32
ROWS = 8
OWN = 2 * ROWS
WIDE = 5 * ROWS
CHUNK = 4
LAGS = 16


def chunks(low, high):
    at = low
    while at < high:
        yield at, min(at + CHUNK, high)
        at += CHUNK


def kernel(intervals, depth, far_initial, far_cond, far_source, out, initial, cond, source, land_s, land_k, land_u, kx, sx, coef_a, coef_c, diag_a, diag_c,
           zed_a, zed_c, ping, pong, gsum, pair_in, v_mine, v_in, base, gam, dif, gam_w, dif_w, mixed, slots, start,
           middle, out_send, sem_s, sem_k, sem_u, sem_h, sem_p, sem_v, sem_m, sem_d, sem_o, sem_i):
    tm = lax.axis_index("tm")
    z = lax.axis_index("space")
    interval = tm // 4
    quarter = tm % 4
    side = quarter // 2
    core = quarter % 2
    block = 2 * z + core
    first = interval == intervals - 1
    item = lax.rem(interval + 1, intervals)
    blocks = 2 * depth
    left = (tm - core + (1 - core), lax.rem(z + depth - (1 - core), depth))
    right = (tm - core + (1 - core), lax.rem(z + core, depth))
    pair_tm = tm - 2 * side + 2 * (1 - side)
    pair = (pair_tm, z)
    cross_tm = pair_tm - core + (1 - core)
    chip_tm = tm - core

    def interval_tm(which):
        return 4 * which + quarter

    fetches = [
        pltpu.make_async_copy(there, here, sem_i.at[k])
        for k, (there, here) in enumerate(((far_cond, cond), (far_source, source), (far_initial, initial)))
    ]
    barrier = pltpu.get_barrier_semaphore()

    def greet(device):
        pl.semaphore_signal(barrier, inc=1, device_id=device, device_id_type=MESH)

    partners = 0
    for step in sorted(range(depth), key=lambda at: -min(at, depth - at)):
        other = lax.rem(z + step, depth)
        greet((tm - core + (1 - core), other))
        partners += 1
        if step:
            greet((tm, other))
            partners += 1
    greet(pair)
    greet((cross_tm, left[1]))
    greet((cross_tm, right[1]))
    partners += 3
    for step in range(1, intervals):
        greet((interval_tm(lax.rem(interval + step, intervals)), z))
        partners += 1
    for fetch in fetches:
        fetch.start()
    for fetch in fetches:
        fetch.wait()
    pl.semaphore_wait(barrier, partners)

    def send(src, dst, sems, k, device):
        pltpu.make_async_remote_copy(
            src_ref=src, dst_ref=dst, send_sem=sems.at[0, k], recv_sem=sems.at[1, k], device_id=device, device_id_type=MESH
        ).start()

    def take(ref, sems, k, way=1):
        pltpu.make_async_copy(ref, ref, sems.at[way, k]).wait()

    def spread(whole, land, sems):
        for step in range(1, depth):
            other = lax.rem(z + step, depth)
            rows = pl.ds(pl.multiple_of((2 * other + core) * ROWS, ROWS), ROWS)
            send(whole.at[:, rows], land.at[z], sems, 0, (tm, other))
        rows = pl.ds(pl.multiple_of(block * ROWS, ROWS), ROWS)
        pltpu.make_async_copy(whole.at[:, rows], land.at[z], sems.at[1, 0]).start()

    spread(cond, land_k, sem_k)
    for step in range(depth):
        other = lax.rem(z + step, depth)
        for flip in range(2):
            if step == 0 and flip == 0:
                continue
            goal = core if flip == 0 else 1 - core
            rows = pl.ds(pl.multiple_of((2 * other + goal) * ROWS, ROWS), ROWS)
            send(source.at[:, :, rows], land_s.at[core * depth + z], sem_s, 0, (chip_tm + goal, other))
    rows = pl.ds(pl.multiple_of(block * ROWS, ROWS), ROWS)
    pltpu.make_async_copy(source.at[:, :, rows], land_s.at[core * depth + z], sem_s.at[1, 0]).start()

    @pl.when(first)
    def _():
        spread(initial, land_u, sem_u)

    def gathered(land, row, parity, base_row, stride):
        flat = land.reshape(land.size // 128, 128)
        return flat[pl.ds(base_row + parity * ROWS + row, 8, stride=stride), :]

    own = pl.ds(OWN, ROWS)
    left2 = (tm, lax.rem(z + depth - 1, depth))
    right2 = (tm, lax.rem(z + 1, depth))

    def halo(field, k, rows):
        send(field.at[pl.ds(OWN, rows)], field.at[pl.ds(OWN + ROWS, rows)], sem_h, k, left)
        send(field.at[pl.ds(OWN + ROWS - rows, rows)], field.at[pl.ds(OWN - rows, rows)], sem_h, k + 1, right)

    def halo_take(field, k, rows, way=1):
        take(field.at[pl.ds(OWN + ROWS, rows)], sem_h, k, way)
        take(field.at[pl.ds(OWN - rows, rows)], sem_h, k + 1, way)

    def wide_halo(field, k):
        for turn, (device, at) in enumerate(((left, 3), (right, 1), (left2, 4), (right2, 0))):
            send(field.at[own], field.at[pl.ds(at * ROWS, ROWS)], sem_h, k + turn, device)

    def wide_take(field, k, way=1):
        for turn, at in enumerate((3, 1, 4, 0)):
            take(field.at[pl.ds(at * ROWS, ROWS)], sem_h, k + turn, way)

    take(land_k, sem_k, 0)
    for row in range(ROWS):
        for parity in range(2):
            kx[OWN + row, parity] = gathered(land_k, row, parity, 0, 2 * ROWS)
    halo(kx, 0, ROWS)

    take(land_s, sem_s, 0)
    for pick in range(4):
        for row in range(ROWS):
            for parity in range(2):
                sx[pick, OWN + row, parity] = gathered(
                    land_s, row, parity, (pick // 2) * depth * 4 * ROWS + (pick % 2) * 2 * ROWS, 4 * ROWS
                )
    for pick in range(4):
        halo(sx.at[pick], 4 + 2 * pick, ROWS - 1 - pick)
    send(kx.at[own], kx.at[pl.ds(4 * ROWS, ROWS)], sem_h, 2, left2)
    send(kx.at[own], kx.at[pl.ds(0, ROWS)], sem_h, 3, right2)

    halo_take(kx, 0, ROWS)
    lane = lax.broadcasted_iota(jnp.int32, (8, 128), 1)
    sub = lax.broadcasted_iota(jnp.int32, (8, 128), 0)
    low_edge = block == 0
    high_edge = block == blocks - 1

    def kof(row, parity):
        value = kx[row, parity]
        if row < OWN:
            value = jnp.where(low_edge if row >= ROWS else block <= 1, F32(0.0), value)
        if row >= OWN + ROWS:
            value = jnp.where(high_edge if row < OWN + 2 * ROWS else block >= blocks - 2, F32(0.0), value)
        return value

    half = F32(0.01)
    zero = F32(0.0)
    def coefficients(row, below):
        k0, k1 = kof(row, 0), kof(row, 1)
        za = half * (k0 + k1)
        zb_all = half * (k1 + jnp.where(sub == 7, zero, pltpu.roll(k0, 7, 0)))
        zb_off = jnp.where(sub == 7, zero, zb_all)
        zc_all = half * (k0 + jnp.where(sub == 0, zero, pltpu.roll(k1, 1, 0)))
        zc_off = jnp.where(sub == 0, zero, zc_all)
        zed_a[row, 0], zed_a[row, 1], zed_a[row, 2] = za, zc_off, zb_off
        zed_c[row, 0], zed_c[row, 1], zed_c[row, 2] = 8.0 * za, 8.0 * zc_off, 8.0 * zb_off
        for parity, here in enumerate((k0, k1)):
            up_all = half * (here + kof(row + 1, parity))
            up_off = up_all
            for edge, at in ((block == 1, 1), (low_edge, 2), (high_edge, 3), (block == blocks - 2, 4)):
                if row == at * ROWS - 1:
                    up_off = jnp.where(edge, zero, up_all)
            yp_all = half * (here + jnp.where(lane == 127, zero, pltpu.roll(here, 127, 1)))
            yp_off = jnp.where(lane == 127, zero, yp_all)
            ym_all = half * (here + jnp.where(lane == 0, zero, pltpu.roll(here, 1, 1)))
            ym_off = jnp.where(lane == 0, zero, ym_all)
            coef_a[0, row, parity], coef_c[0, row, parity] = up_off, 8.0 * up_off
            if below:
                down_all = half * (here + kof(row - 1, parity))
                total = (za + (zc_all if parity == 0 else zb_all)) + (yp_all + ym_all) + (up_all + down_all)
                coef_a[1, row, parity], coef_c[1, row, parity] = yp_off, 8.0 * yp_off
                coef_a[2, row, parity], coef_c[2, row, parity] = ym_off, 8.0 * ym_off
                diag_a[row, parity], diag_c[row, parity] = 1.0 - total, 1.0 - 8.0 * total

    for row in range(ROWS, 4 * ROWS - 1):
        coefficients(row, row > ROWS)

    fine = (coef_a, diag_a, zed_a)
    coarse = (coef_c, diag_c, zed_c)

    def stencil(ops, src, a, b):
        coef, diag, zed = ops
        n = b - a
        here = [src[pl.ds(a, n), parity] for parity in range(2)]
        outs = []
        for parity in range(2):
            u = here[parity]
            across = here[1 - parity]
            turned = pltpu.roll(across, 1 if parity == 0 else 7, 1)
            vert = zed[pl.ds(a, n), 0] * across + zed[pl.ds(a, n), 1 + parity] * turned
            rows = coef[0, pl.ds(a, n), parity] * src[pl.ds(a + 1, n), parity] \
                + coef[0, pl.ds(a - 1, n), parity] * src[pl.ds(a - 1, n), parity]
            cols = coef[1, pl.ds(a, n), parity] * pltpu.roll(u, 127, 2) + coef[2, pl.ds(a, n), parity] * pltpu.roll(u, 1, 2)
            outs.append((diag[pl.ds(a, n), parity] * u + rows) + (vert + cols))
        return outs

    def apply(ops, src, dst, low, high, forcing=None):
        for a, b in chunks(low, high):
            outs = stencil(ops, src, a, b)
            for parity in range(2):
                value = outs[parity]
                if forcing is not None:
                    value = value + forcing[pl.ds(a, b - a), parity]
                dst[pl.ds(a, b - a), parity] = value

    def run(ops, src, dst, steps, reach, spare):
        current = src
        for step in range(steps):
            reach -= 1
            goal = dst if step == steps - 1 else spare[step % 2]
            apply(ops, current, goal, OWN - reach, OWN + ROWS + reach)
            current = goal

    spare = (ping, pong)

    for pick in range(2):
        halo_take(sx.at[pick], 4 + 2 * pick, ROWS - 1 - pick)
    apply(fine, sx.at[0], ping, OWN - 6, OWN + ROWS + 6, sx.at[1])
    halo_take(sx.at[2], 8, ROWS - 3)
    apply(fine, ping, pong, OWN - 5, OWN + ROWS + 5, sx.at[2])
    halo_take(sx.at[3], 10, ROWS - 4)
    apply(fine, pong, v_mine, OWN - 4, OWN + ROWS + 4, sx.at[3])
    run(fine, v_mine, gsum, 4, 4, spare)

    @pl.when(side == 1)
    def _():
        gsum[own] = v_mine[own]

    @pl.when(first)
    def _():
        take(land_u, sem_u, 0)
        for row in range(ROWS):
            for parity in range(2):
                gsum[OWN + row, parity] = jnp.where(side == 0, gathered(land_u, row, parity, 0, 2 * ROWS), zero)

    send(gsum.at[own], pair_in.at[own], sem_p, 0, pair)
    take(kx.at[pl.ds(4 * ROWS, ROWS)], sem_h, 2)
    take(kx.at[pl.ds(0, ROWS)], sem_h, 3)
    for row in (*range(ROWS + 1), *range(4 * ROWS - 1, WIDE - 1)):
        coefficients(row, row > 0)
    take(pair_in.at[own], sem_p, 0)
    base[0, own] = gsum[own] + pair_in[own]
    wide_halo(base.at[0], 12)

    mine = pl.ds(OWN + 4 * side, 4)

    def post(n, src):
        @pl.when(item + n < intervals)
        def _():
            send(src, slots.at[n], sem_m, n, (interval_tm(item + n), z))

    post(0, base.at[0, mine])
    wide_take(base.at[0], 12)
    run(fine, base.at[0], base.at[1], 8, 16, spare)
    post(1, base.at[1, mine])
    run(fine, base.at[1], base.at[2], 8, 8, spare)
    wide_halo(base.at[2], 16)
    post(2, base.at[2, mine])

    @pl.when(side == 0)
    def _():
        send(v_mine.at[pl.ds(OWN - 4, 16)], v_in.at[pl.ds(OWN - 4, 16)], sem_v, 0, pair)

    wide_take(base.at[2], 16)
    apply(coarse, base.at[2], dif.at[0], OWN - ROWS, OWN + 2 * ROWS)
    run(fine, base.at[2], gam.at[0], 8, 16, spare)
    inner_rows = pl.ds(OWN - ROWS, 3 * ROWS)
    dif[0, inner_rows] = gam[0, inner_rows] - dif[0, inner_rows]

    for turn in range(13):
        at, inner = turn // 8, turn % 8
        if inner == 0:
            now_g, now_d = gam.at[at], dif.at[at]
            reach = 8
            if at:
                reach = 4
                halo(now_d, 22, reach)
        if turn == 0:
            post(3, now_g.at[mine])
        else:
            mixed[turn] = now_g[mine] + F32(turn) * now_d[mine]
            if turn < 12:
                post(3 + turn, mixed.at[turn])
        if inner == 0 and at:
            halo_take(now_g, 20, reach)
            halo_take(now_d, 22, reach)
        if turn == 12:
            break
        reach -= 1
        last = inner == 7
        next_g = gam.at[at + 1] if last else gam_w.at[inner % 2]
        next_d = dif.at[at + 1] if last else dif_w.at[inner % 2]
        apply(coarse, now_g, next_g, OWN - reach, OWN + ROWS + reach)
        if last:
            halo(next_g, 20, 4)
        apply(coarse, now_d, next_d, OWN - reach, OWN + ROWS + reach)
        now_g, now_d = next_g, next_d

    start[mine] = jnp.where(first, mixed[12], jnp.zeros_like(mixed[12]))
    for n in range(LAGS - 1):
        @pl.when(n <= interval)
        def _():
            take(slots.at[n], sem_m, n)
            start[mine] = start[mine] + slots[n]

    below = pl.ds(OWN - ROWS + 4 * side, 4)
    above = pl.ds(OWN + ROWS + 4 * side, 4)
    send(start.at[mine], start.at[mine], sem_d, 0, pair)
    send(start.at[mine], start.at[above], sem_d, 1, left)
    send(start.at[mine], start.at[below], sem_d, 2, right)
    send(start.at[mine], start.at[above], sem_d, 3, (cross_tm, left[1]))
    send(start.at[mine], start.at[below], sem_d, 4, (cross_tm, right[1]))
    for k in range(5):
        take(slots.at[0], sem_d, k)

    run(fine, start, middle, 4, 8, spare)

    @pl.when(side == 0)
    def _():
        middle[pl.ds(OWN - 4, 16)] = start[pl.ds(OWN - 4, 16)]

    @pl.when(side == 1)
    def _():
        take(v_in.at[pl.ds(OWN - 4, 16)], sem_v, 0)
        middle[pl.ds(OWN - 4, 16)] = middle[pl.ds(OWN - 4, 16)] + v_in[pl.ds(OWN - 4, 16)]

    flat = out_send.reshape(out_send.size // 128, 128)
    current = middle
    my_rows = pl.ds(pl.multiple_of(block * ROWS, ROWS), ROWS)
    for pick in range(4):
        goal = spare[pick % 2]
        reach = 3 - pick
        apply(fine, current, goal, OWN - reach, OWN + ROWS + reach, sx.at[pick])
        current = goal
        origin = (pick // 2) * depth * 4 * ROWS + (pick % 2) * 2 * ROWS
        for row in range(ROWS):
            for parity in range(2):
                flat[pl.ds(origin + parity * ROWS + row, 8, stride=4 * ROWS), :] = goal[OWN + row, parity]
        if pick % 2:
            goal_core = pick // 2
            for step in (4, 3, 5, 2, 6, 1, 7):
                other = lax.rem(z + step, depth)
                send(out_send.at[goal_core, other], out.at[:, :, my_rows], sem_o, 0, (chip_tm + goal_core, other))

            @pl.when(core == goal_core)
            def _():
                pltpu.make_async_copy(out_send.at[goal_core, z], out.at[:, :, my_rows], sem_o.at[1, 0]).start()

            @pl.when(core != goal_core)
            def _():
                send(out_send.at[goal_core, z], out.at[:, :, my_rows], sem_o, 0, (chip_tm + goal_core, z))

    take(land_k.at[pl.ds(0, depth - 1)], sem_k, 0, 0)
    take(land_s.at[pl.ds(0, 2 * depth - 1)], sem_s, 0, 0)

    @pl.when(first)
    def _():
        take(land_u.at[pl.ds(0, depth - 1)], sem_u, 0, 0)

    @pl.when(side == 0)
    def _():
        take(v_in.at[pl.ds(OWN - 4, 16)], sem_v, 0, 0)

    wide_take(kx, 0, 0)
    for pick in range(4):
        halo_take(sx.at[pick], 4 + 2 * pick, ROWS - 1 - pick, 0)
    take(gsum.at[own], sem_p, 0, 0)
    wide_take(base.at[0], 12, 0)
    wide_take(base.at[2], 16, 0)
    halo_take(gam.at[1], 20, 4, 0)
    halo_take(dif.at[1], 22, 4, 0)
    for n in range(LAGS - 1):
        @pl.when(item + n < intervals)
        def _():
            take(slots.at[n], sem_m, n, 0)
    for k in range(5):
        take(slots.at[0], sem_d, k, 0)
    take(land_s.at[pl.ds(0, 2 * depth - 1)], sem_o, 0, 0)
    take(out, sem_o, 0)


def local(intervals, depth, initial, cond, source):
    def vm(*shape):
        return pltpu.VMEM(shape, F32)

    def field(*lead):
        return vm(*lead, WIDE, 2, 8, 128)

    dma = pltpu.SemaphoreType.DMA
    return pl.pallas_call(
        functools.partial(kernel, intervals, depth),
        out_shape=jax.ShapeDtypeStruct(source.shape, F32),
        in_specs=[pl.BlockSpec(memory_space=pl.ANY)] * 3,
        out_specs=pl.BlockSpec(memory_space=pl.ANY),
        scratch_shapes=[
            vm(*initial.shape),
            vm(*cond.shape),
            vm(*source.shape),
            vm(2 * depth, 2, 2, ROWS, 128),
            vm(depth, 2, ROWS, 128),
            vm(depth, 2, ROWS, 128),
            field(),
            field(4),
            field(3),
            field(3),
            field(),
            field(),
            vm(WIDE, 3, 8, 128),
            vm(WIDE, 3, 8, 128),
            field(),
            field(),
            field(),
            field(),
            field(),
            field(),
            field(3),
            field(2),
            field(2),
            field(2),
            field(2),
            vm(13, 4, 2, 8, 128),
            vm(LAGS, 4, 2, 8, 128),
            field(),
            field(),
            vm(2, depth, 2, 2, ROWS, 128),
            dma((2, 1)),
            dma((2, 1)),
            dma((2, 1)),
            dma((2, 24)),
            dma((2, 5)),
            dma((2, 1)),
            dma((2, LAGS)),
            dma((2, 5)),
            dma((2, 1)),
            dma((3,)),
        ],
        compiler_params=pltpu.CompilerParams(
            collective_id=0, has_side_effects=True, vmem_limit_bytes=60 * 1024 * 1024
        ),
        name="mgrit",
    )(initial, cond, source)


def solution(mesh):
    intervals = mesh.shape["tm"] // 4
    depth = mesh.shape["space"]
    return jax.shard_map(
        functools.partial(local, intervals, depth),
        mesh=mesh,
        in_specs=(P("space", None, None), P("space", None, None), P("tm", "space", None, None)),
        out_specs=P("tm", "space", None, None),
        check_vma=False,
    )
```
